32 devices in a mesh: groups: 2 (over y), mp: 4 (over z), role: 2 (over core), rep: 2 (over x).
Axes of the slice: x: 2, y: 2, z: 4, core: 2. Of those that a mesh axis runs over, the one named last changes fastest.
Arguments:
- teacher_rows: bfloat16 [5120, 8192], P(('groups', 'mp', 'role'), 'rep'), parts along dimension 0, may hold values from -1400 to 1400
- teacher_gain: float32 [8192], P('rep'), may hold values from 0.5 to 2
- teacher_value: bfloat16 [8192, 1024], P('rep', 'role'), may hold values from -0.0625 to 0.0625
- student_rows: bfloat16 [10240, 5120], P(('groups', 'mp', 'role'), 'rep'), parts along dimension 0, may hold values from -1400 to 1400
- student_gain: float32 [5120], P('rep'), may hold values from 0.5 to 2
- student_value: bfloat16 [5120, 1024], P('rep', 'role'), may hold values from -0.078125 to 0.078125
- owners: int32 [5120, 1], P(('groups', 'mp', 'role')), parts along dimension 0, may hold values from 0 to 7; in each aligned block of 320 rows (0 to 319, 320 to 639, ...) at most 80 rows name the same one
Outputs:
- value_error: bfloat16 [10240, 1024], P(('groups', 'mp', 'role'), 'rep'), parts along dimension 0
- grad_value: float32 [10240, 1024], P(('groups', 'rep'), 'role'), parts along dimension 0
The draws below stay inside these ranges and needn't reach their ends.
There are 2 independent parts, one for each index of `groups`. The reference program is written for one: setup_inputs(seed, part) draws one part's arguments, and reference() takes and returns one part's arrays. A program takes and returns all parts, laid end to end along the dimension named above; an argument that names none is the same for every part. Nothing has to cross between parts.
Inputs may be any that keep to these rules, and one draw needn't show every extreme that they name: `owners`: in each aligned block of 320 rows (the rows of one index of mp and role), no student shard is named by more than 80 rows, a bound that some block reaches.
All inputs are finite; a program needn't handle non-finite values.
Results may differ from the reference program's by a relative error of at most 0.012.
Values may be sent and summed in bfloat16 or wider, within the bound.
A program may use at most 128 MiB of HBM per device.

```python
import math
import jax
import jax.numpy as jnp
import numpy as np
from jax import lax

DT = 8192
DS = 5120
KV = 1024
TB = 320
SLOT = 80
TOKENS = 2560
SLOTS = 5120
N_MP = 4
N_ROLE = 2


def spread_rows(key, rows_count, width, top):
    keys = jax.random.split(key, 5)
    normal_part = jnp.clip(jax.random.normal(keys[0], (rows_count, width), jnp.float32), -5.0, 5.0)
    base = normal_part
    column_scale = jnp.exp(2.302585 * jnp.arange(width, dtype=jnp.float32) / width)
    column_scale = column_scale[None, :] * jax.random.uniform(keys[3], (1, width), jnp.float32, 0.7, 1.4)
    rows_scale = jnp.exp(jax.random.uniform(keys[4], (rows_count, 1), jnp.float32, 0.0, 1.0) * jnp.log(top))
    return (base * column_scale * rows_scale).astype(jnp.bfloat16)


def draw_teacher_rows(key, part):
    key = jax.random.fold_in(key, 11)
    return spread_rows(key, TOKENS, DT, 10.0)


def draw_student_rows(key, part):
    key = jax.random.fold_in(key, 23)
    return spread_rows(key, SLOTS, DS, 10.0)


def level_of(stream_key, shape, pieces, low, top_value):
    gain, own = 1.0, jax.random.fold_in(stream_key, 6)
    for position, parts in pieces:
        draws = jnp.exp(jax.random.uniform(jax.random.fold_in(own, position), (parts,), jnp.float32, low / len(pieces), top_value / len(pieces)))
        gain = gain * jnp.repeat(draws, shape[position] // parts).reshape([-1 if axis == position else 1 for axis in range(len(shape))])
    return gain


def routed_block(stream_key, own, number, rows, amount, top, reach, skew):
    sequence = jax.random.permutation(stream_key, amount)
    crowded, ordinary = portions_of(amount, rows * top, reach, skew, True), portions_of(amount, rows * top, reach, skew, False)
    places = jnp.arange(amount)

    def named(sizes, turn):
        used = int((sizes > 0).sum())
        fixed = max(1, used // 4)
        shifted = fixed + (places - fixed + turn * (used - fixed)) % max(1, amount - fixed)
        return jnp.zeros((amount,), jnp.int32).at[sequence[jnp.where(places < fixed, places, shifted)]].set(jnp.asarray(sizes, jnp.int32))

    sizes = jnp.where(number % 4 == 0, named(crowded, number // 4), named(ordinary, number - number // 4 - 1))
    mixed = jax.random.permutation(jax.random.fold_in(own, 3), amount)
    giver, receiver = mixed[0:amount // 2 * 2:2], mixed[1:amount // 2 * 2:2]
    slack = jnp.minimum(sizes[giver] - 1, reach - sizes[receiver]) // 2
    slack = jnp.where((giver == sequence[0]) | (receiver == sequence[0]) | (sizes[receiver] == 0), 0, jnp.maximum(slack, 0))
    shifted = jax.random.randint(jax.random.fold_in(own, 4), (amount // 2,), 0, 1 << 20) % (slack + 1)
    sizes = sizes.at[giver].add(-shifted).at[receiver].add(shifted)
    labels = jnp.searchsorted(jnp.cumsum(sizes), jnp.arange(rows * top), side="right").astype(jnp.int32)
    listing = labels.reshape(top, rows).T
    listing = listing[jax.random.permutation(jax.random.fold_in(own, 1), rows)]
    turn = jax.random.randint(jax.random.fold_in(own, 2), (rows, 1), 0, top)
    return jnp.take_along_axis(listing, (jnp.arange(top)[None, :] + turn) % top, axis=1)


def portions_of(count, total, limit, lean, full):
    weights = [(1 << 20) // math.isqrt(standing ** lean) + 1 for standing in range(1, count + 1)]
    largest = limit if full else min(limit, max(-(-total // count), total * weights[0] // sum(weights)))
    least = 1 if total - largest >= count - 1 else 0
    counts, surplus = [largest] + [least] * (count - 1), total - largest - least * (count - 1)
    while surplus > 0:
        candidates = [i for i in range(1, count) if counts[i] < largest] or [i for i in range(1, count) if counts[i] < limit]
        pool, left = sum([weights[i] for i in candidates]), surplus
        for i in candidates:
            more = min(limit - counts[i], max(1, left * weights[i] // pool), surplus)
            counts[i] = counts[i] + more
            surplus = surplus - more
    return np.array(counts)


def gaussian(stream_key, shape, deviation, limit, pieces=(), held_as=jnp.bfloat16):
    array = jax.random.normal(stream_key, shape, jnp.float32) * deviation
    if len(pieces) > 0:
        array = level_of(stream_key, shape, pieces, -0.22, 0.18) * array
    return jnp.clip(array, min=-limit, max=limit).astype(held_as)


def setup_inputs(seed: int = 0, part: int = 0) -> dict:
    seeds = jax.random.split(jax.random.key(seed), 8)
    part_keys = jax.random.split(jax.random.fold_in(seeds[7], part), 8)
    teacher_rows = draw_teacher_rows(jax.random.fold_in(jax.random.fold_in(seeds[7], part), 71), part)
    teacher_gain = jnp.clip(jnp.exp(math.log(2.0) - 1.3862944 * jax.random.uniform(seeds[1], (DT,), jnp.float32) ** level_of(seeds[1], (DT,), ((0, 2),), -0.2, 0.2)), 0.5, 2.0)
    teacher_value = gaussian(seeds[2], (DT, KV), DT ** -0.5, 0.0625, ((0, 2), (1, 2)))
    student_rows = draw_student_rows(jax.random.fold_in(jax.random.fold_in(seeds[7], part), 71), part)
    student_gain = jnp.clip(jnp.exp(math.log(2.0) - 1.3862944 * jax.random.uniform(seeds[4], (DS,), jnp.float32) ** level_of(seeds[4], (DS,), ((0, 2),), -0.2, 0.2)), 0.5, 2.0)
    student_value = gaussian(seeds[5], (DS, KV), DS ** -0.5, 0.078125, ((0, 2), (1, 2)))
    owners_keys = jax.random.split(jax.random.fold_in(part_keys[6], 1), TOKENS // TB)
    owners_turns = jax.random.permutation(jax.random.fold_in(part_keys[6], 3), TOKENS // TB)
    owners = jax.vmap(lambda own, number: routed_block(jax.random.fold_in(part_keys[6], 2), own, number, TB, N_MP * N_ROLE, 1, SLOT, 2))(owners_keys, owners_turns).reshape((TOKENS, 1))
    return dict(teacher_rows=teacher_rows, teacher_gain=teacher_gain, teacher_value=teacher_value, student_rows=student_rows, student_gain=student_gain, student_value=student_value, owners=owners)


EPS = 1e-06

def row_scale(rows_in, width):
    widened = rows_in.astype(jnp.float32)
    return lax.rsqrt(lax.optimization_barrier(jnp.sum(widened * widened, axis=1)) / width + EPS)

def reference(teacher_rows, teacher_gain, teacher_value, student_rows, student_gain, student_value, owners):
    peer_count = N_MP * N_ROLE
    teacher_gated = (teacher_rows.astype(jnp.float32) * teacher_gain[None, :]).astype(jnp.bfloat16)
    teacher_scale = row_scale(teacher_rows, DT)
    teacher_sum = jnp.dot(teacher_gated, teacher_value, preferred_element_type=jnp.float32)
    teacher_values = (teacher_sum * teacher_scale[:, None]).astype(jnp.bfloat16)
    student_gated = (student_rows.astype(jnp.float32) * student_gain[None, :]).astype(jnp.bfloat16)
    student_scale = row_scale(student_rows, DS)
    student_values = jnp.dot(student_gated, student_value, preferred_element_type=jnp.float32) * student_scale[:, None]
    owner_col = owners[:, 0].reshape(peer_count, TB)
    everyone = jnp.arange(peer_count, dtype=jnp.int32)
    onehot = (owner_col[:, :, None] == everyone[None, None, :]).astype(jnp.int32)
    rank_in = lax.optimization_barrier(jnp.sum((jnp.cumsum(onehot, axis=1) - onehot) * onehot, axis=2))
    blocks = jnp.arange(peer_count, dtype=jnp.int32)[:, None]
    dest_slot = (owner_col * (peer_count * SLOT) + blocks * SLOT + rank_in).reshape(-1).astype(jnp.int32)
    total_slots = peer_count * peer_count * SLOT
    target = jnp.zeros((total_slots, KV), jnp.bfloat16).at[dest_slot].set(teacher_values)
    live_slot = jnp.zeros((total_slots,), jnp.float32).at[dest_slot].set(1.0)
    value_gap = (student_values - target.astype(jnp.float32)) * live_slot[:, None]
    value_error = value_gap.astype(jnp.bfloat16)
    cotangent = (value_gap * student_scale[:, None] * (1.0 / math.sqrt(TOKENS))).astype(jnp.bfloat16)
    grad_value = jnp.dot(student_gated.T, cotangent, preferred_element_type=jnp.float32)
    return (value_error, grad_value)
```

```python
import math

import jax
import jax.numpy as jnp
from jax import lax
from jax.experimental import pallas as pl
from jax.experimental.pallas import tpu as pltpu
from jax.sharding import PartitionSpec as P

DT = 8192
DS = 5120
KV = 1024


EPS = 1e-06


def squares_of(rows_in):
    widened = rows_in.astype(jnp.float32)
    return jnp.sum(widened * widened, axis=1)


def shards(
    teacher_rows, teacher_gain, teacher_value, student_rows, student_gain, student_value, owners
):
    peer_count = lax.axis_size(("mp", "role"))
    block_rows = teacher_rows.shape[0]
    slot_cap = student_rows.shape[0] // peer_count
    teacher_full, student_full = (
        lax.all_gather(teacher_value, "role", axis=1, tiled=True),
        lax.all_gather(student_value, "role", axis=1, tiled=True),
    )
    teacher_gated = (teacher_rows.astype(jnp.float32) * teacher_gain[None, :]).astype(jnp.bfloat16)
    student_gated = (student_rows.astype(jnp.float32) * student_gain[None, :]).astype(jnp.bfloat16)
    teacher_squares, student_squares = lax.psum(
        (squares_of(teacher_rows), squares_of(student_rows)), "rep"
    )
    teacher_scale = lax.rsqrt(teacher_squares / DT + EPS)
    student_scale = lax.rsqrt(student_squares / DS + EPS)
    teacher_part = jnp.dot(teacher_gated, teacher_full, preferred_element_type=jnp.float32)
    student_part = jnp.dot(student_gated, student_full, preferred_element_type=jnp.float32)
    teacher_sum, student_sum = (
        lax.psum_scatter(teacher_part, "rep", scatter_dimension=1, tiled=True),
        lax.psum_scatter(student_part, "rep", scatter_dimension=1, tiled=True),
    )
    teacher_values = (teacher_sum * teacher_scale[:, None]).astype(jnp.bfloat16)
    student_values = student_sum * student_scale[:, None]
    owner_col = owners[:, 0]
    all_owners = lax.all_gather(owner_col, ("mp", "role"), axis=0, tiled=True).reshape(
        peer_count, block_rows
    )
    myself = lax.axis_index(("mp", "role"))
    is_mine = (all_owners == myself).astype(jnp.int32)
    counts = jnp.sum(is_mine, axis=1)
    live_slot = (jnp.arange(slot_cap, dtype=jnp.int32)[None, :] < counts[:, None]).reshape(-1)
    every_row = lax.all_gather(teacher_values, ("mp", "role"), axis=0, tiled=True)
    rank_in = jnp.cumsum(is_mine, axis=1) - is_mine
    blocks = jnp.arange(peer_count, dtype=jnp.int32)[:, None]
    where_to = jnp.where(is_mine > 0, blocks * slot_cap + rank_in, peer_count * slot_cap)
    source = blocks * block_rows + jnp.arange(block_rows, dtype=jnp.int32)[None, :]
    pick_rows = (
        jnp.zeros((peer_count * slot_cap,), jnp.int32)
        .at[where_to.reshape(-1)]
        .set(source.reshape(-1), mode="drop")
    )
    target = jnp.take(every_row, pick_rows, axis=0)
    value_gap = jnp.where(live_slot[:, None], student_values - target.astype(jnp.float32), 0.0)
    value_error = value_gap.astype(jnp.bfloat16)
    tokens = peer_count * block_rows
    cotangent = (value_gap * student_scale[:, None] * (1.0 / math.sqrt(tokens))).astype(
        jnp.bfloat16
    )
    cotangent_full = lax.all_gather(cotangent, "rep", axis=1, tiled=True)
    half_cols = KV // lax.axis_size("role")
    role_index = lax.axis_index("role")
    grad_part = lax.dot_general(
        student_gated, cotangent_full, (((0,), (0,)), ((), ())), preferred_element_type=jnp.float32
    )
    grad_total = lax.psum(grad_part.astype(jnp.bfloat16), ("mp", "role")).astype(jnp.float32)
    grad_value = lax.dynamic_slice_in_dim(grad_total, role_index * half_cols, half_cols, 1)
    return (value_error, grad_value)


MESH = pl.DeviceIdType.MESH
SENTINEL = 1048576.0


def fused(
    t_hbm, tg_ref, tw_hbm, s_hbm, sg_ref, sw_hbm, ow_ref,
    err_ref, grad_ref,
    tr, sr, tw, sw, ow, gt, tp, sp, tsq, ssq, tx_out, tx_in, sx_out, sx_in,
    tq_out, tq_in, sq_out, sq_in, pk, tgt, gap, gap_half, cot, part_out, outer_in, mid_in,
    lsem, sib_s, sib_r, x_s, x_r, q_s, q_r, z_s, z_r, g_s, g_r, v_s, v_r,
    a_s, a_r, b_s, b_r, c_s, c_r,
):
    g, m = lax.axis_index("groups"), lax.axis_index("mp")
    r, x = lax.axis_index("role"), lax.axis_index("rep")
    blk, tk = t_hbm.shape
    slots, sk = s_hbm.shape
    cols = tw_hbm.shape[1]
    half = cols // 2
    n_mp = lax.axis_size("mp")
    cap = slots // (2 * n_mp)
    tokens = blk * 2 * n_mp
    sib = (g, m, 1 - r, x)
    xp = (g, m, r, 1 - x)

    def z_dev(k):
        return (g, lax.rem(m + k, n_mp), r, x)

    peers = [sib, xp] + [z_dev(k) for k in range(1, n_mp)]
    barrier = pltpu.get_barrier_semaphore()
    for d in peers:
        pl.semaphore_signal(barrier, inc=1, device_id=d, device_id_type=MESH)

    loc = [
        pltpu.make_async_copy(t_hbm, tr.at[r], lsem.at[0]),
        pltpu.make_async_copy(tw_hbm, tw, lsem.at[1]),
        pltpu.make_async_copy(s_hbm, sr.at[r], lsem.at[2]),
        pltpu.make_async_copy(sw_hbm, sw, lsem.at[3]),
        pltpu.make_async_copy(ow_ref, ow.at[r], lsem.at[4]),
    ]
    for c in loc:
        c.start()
    pl.semaphore_wait(barrier, len(peers))

    def remote(src, dst, ss, rs, dev):
        return pltpu.make_async_remote_copy(
            src_ref=src, dst_ref=dst, send_sem=ss, recv_sem=rs, device_id=dev, device_id_type=MESH
        )

    sib_t = remote(t_hbm, tr.at[r], sib_s.at[0], sib_r.at[0], sib)
    sib_o = remote(ow_ref, ow.at[r], sib_s.at[1], sib_r.at[1], sib)
    sib_x = remote(s_hbm, sr.at[r], sib_s.at[2], sib_r.at[2], sib)
    sib_t.start()
    sib_o.start()
    sib_x.start()

    keep = pl.ds(pl.multiple_of(x * half, half), half)
    give = pl.ds(pl.multiple_of((1 - x) * half, half), half)

    def square_lanes(v):
        v = v * v
        total = v[:, 0:128]
        for j in range(1, v.shape[1] // 128):
            total = total + v[:, j * 128 : (j + 1) * 128]
        return total

    rt = 64

    def project(src, b, dst, out, gain, w, sq, depth, kt):
        rows = src.shape[1]
        sq[...] = jnp.zeros_like(sq)
        out[...] = jnp.zeros_like(out)

        @pl.loop(0, depth // kt)
        def _(k):
            ks = pl.ds(pl.multiple_of(k * kt, kt), kt)
            gain_k = gain[:, ks]

            @pl.loop(0, rows // rt)
            def _(i):
                rs = pl.ds(pl.multiple_of(i * rt, rt), rt)
                v = src[b, rs, ks].astype(jnp.float32)
                sq[rs, :] += square_lanes(v)
                if dst is None:
                    src[b, rs, ks] = (v * gain_k).astype(jnp.bfloat16)
                else:
                    dst[rs, :] = (v * gain_k).astype(jnp.bfloat16)

            gated = src[b, :, ks] if dst is None else dst[...]
            out[...] += jnp.dot(gated, w[ks, :], preferred_element_type=jnp.float32)

    def send_half(out, stage_out, stage_in, sq, q_out, q_in, slot):
        stage_out[slot] = out[:, give].astype(jnp.bfloat16)
        q_out[slot] = jnp.broadcast_to(
            jnp.sum(sq[...].T, axis=0, keepdims=True), q_out.shape[1:]
        )
        return stage_out, q_out

    def x_pair(stage_out, stage_in, q_out, q_in, slot, n):
        return (
            remote(stage_out.at[slot], stage_in.at[slot], x_s.at[n], x_r.at[n], xp),
            remote(q_out.at[slot], q_in.at[slot], q_s.at[n], q_r.at[n], xp),
        )

    t_copies = []
    for step in range(2):
        b = r if step == 0 else 1 - r
        if step == 0:
            loc[0].wait()
            loc[1].wait()
        else:
            sib_t.wait_recv()
        project(tr, b, gt, tp.at[step], tg_ref, tw, tsq, tk, 512)
        send_half(tp.at[step], tx_out, tx_in, tsq, tq_out, tq_in, step)
        pair = x_pair(tx_out, tx_in, tq_out, tq_in, step, step)
        for c in pair:
            c.start()
        t_copies.append(pair)

    s_copies = []

    def student(step):
        b = r if step == 0 else 1 - r
        if step == 0:
            loc[2].wait()
            loc[3].wait()
        else:
            sib_x.wait_recv()
        project(sr, b, None, sp.at[step], sg_ref, sw, ssq, sk, 512)
        send_half(sp.at[step], sx_out, sx_in, ssq, sq_out, sq_in, step)
        pair = x_pair(sx_out, sx_in, sq_out, sq_in, step, 2 + step)
        for c in pair:
            c.start()
        s_copies.append(pair)

    def column(row):
        n = row.shape[1]
        return jnp.broadcast_to(row, (128, n)).T

    student(0)
    loc[4].wait()
    sib_o.wait_recv()
    n_own = 2 * n_mp
    wide = ow.shape[2]
    for step in range(2):
        for c in t_copies[step]:
            c.wait_recv()
        b = r if step == 0 else 1 - r
        sq_sum = tq_out[step, 0:1, :] + tq_in[step, 0:1, :]
        scale = column(lax.rsqrt(sq_sum / DT + EPS))[0:blk]
        scale = jnp.concatenate([scale] * (half // 128), axis=1)
        values = tp[step, :, keep] + tx_in[step].astype(jnp.float32)
        values = (values * scale).astype(jnp.bfloat16)
        own = ow[b]
        eq = (own == lax.broadcasted_iota(jnp.int32, (8, wide), 0)).astype(jnp.float32)
        upper = (
            lax.broadcasted_iota(jnp.int32, (wide, wide), 0)
            < lax.broadcasted_iota(jnp.int32, (wide, wide), 1)
        ).astype(jnp.float32)
        before = jnp.dot(
            eq.astype(jnp.bfloat16), upper.astype(jnp.bfloat16), preferred_element_type=jnp.float32
        )
        rank = jnp.sum(eq * before, axis=0, keepdims=True)
        dest = own[0:1, :].astype(jnp.float32) * cap + rank
        for o in range(n_own // 2):
            spot = lax.broadcasted_iota(jnp.int32, (2 * cap, wide), 0) + o * 2 * cap
            hit = (spot.astype(jnp.float32) == dest).astype(jnp.float32)
            filled = jnp.sum(hit, axis=1, keepdims=True)
            moved = jnp.dot(
                hit[:, 0:blk].astype(jnp.bfloat16), values, preferred_element_type=jnp.float32
            )
            moved = jnp.where(filled > 0.5, moved, SENTINEL).astype(jnp.bfloat16)
            pk[2 * o, b] = moved[0:cap]
            pk[2 * o + 1, b] = moved[cap:]
    z_copies = []
    for k in range(1, n_mp):
        to = lax.rem(m + k, n_mp)
        c = remote(pk.at[pl.ds(2 * to, 2)], tgt.at[:, m], z_s.at[k - 1], z_r.at[k - 1], z_dev(k))
        c.start()
        z_copies.append(c)
    tgt[0, m] = pk[2 * m]
    tgt[1, m] = pk[2 * m + 1]

    student(1)
    for step in range(2):
        for c in s_copies[step]:
            c.wait_recv()
    for c in z_copies:
        c.wait_recv()

    norm = 1.0 / math.sqrt(tokens)
    gap_copies = []
    for step in range(2):
        b = r if step == 0 else 1 - r
        sq_sum = sq_out[step, 0:1, :] + sq_in[step, 0:1, :]
        scale = column(lax.rsqrt(sq_sum / DS + EPS))
        per = 2 * cap
        for s in range(n_mp):
            rs = slice(s * per, (s + 1) * per)
            sc = jnp.concatenate([scale[rs]] * (half // 128), axis=1)
            vals = (sp[step, rs, keep] + sx_in[step, rs].astype(jnp.float32)) * sc
            target = tgt[b, s].reshape(per, half).astype(jnp.float32)
            diff = jnp.where(target < 0.5 * SENTINEL, vals - target, 0.0)
            gap_half[b, rs] = diff.astype(jnp.bfloat16)
            cot[b, rs] = (diff * sc * norm).astype(jnp.bfloat16)
        c = remote(gap_half.at[b], gap.at[b], g_s.at[step], g_r.at[step], xp)
        c.start()
        gap_copies.append(c)
        sp[step, :, 0:128] = scale

    fb = 256
    n_f = sk // fb
    outer = (m == 0) | (m == n_mp - 1)
    inward = jnp.where(m < n_mp // 2, m + 1, m - 1)
    outward = jnp.where(m < n_mp // 2, m - 1, m + 1)
    near = (g, jnp.where(outer, inward, outward), r, x)
    across = (g, inward, r, x)
    n_c = 2 * n_f

    def up(i):
        return remote(part_out.at[i], outer_in.at[i], a_s.at[i], a_r.at[i], near)

    def cross(i):
        return remote(part_out.at[i], mid_in.at[i], b_s.at[i], b_r.at[i], across)

    def place(i):
        f = lax.rem(i, n_f)
        h = jnp.where(i < n_f, x, 1 - x)
        return (
            pl.ds(pl.multiple_of(f * fb, fb), fb),
            pl.ds(pl.multiple_of(h * half, half), half),
        )

    def down(i):
        spot = grad_ref.at[place(i)]
        return remote(spot, spot, c_s.at[i], c_r.at[i], near)

    def grad_part(i):
        f = lax.rem(i, n_f)
        fs = pl.ds(pl.multiple_of(f * fb, fb), fb)
        total = None
        for b in range(2):
            term = lax.dot_general(
                sr[b, :, fs], cot[b], (((0,), (0,)), ((), ())), preferred_element_type=jnp.float32
            )
            total = term if total is None else total + term
        return total

    def finish(i):
        cross(i).wait_recv()
        both = part_out[i].astype(jnp.float32) + mid_in[i].astype(jnp.float32)
        grad_ref[place(i)] = both.astype(jnp.bfloat16)
        down(i).start()

    def chunk(i):
        mine = grad_part(i)

        @pl.when(outer)
        def _():
            part_out[i] = mine.astype(jnp.bfloat16)
            up(i).start()

        @pl.when(jnp.logical_not(outer))
        def _():
            up(i).wait_recv()
            part_out[i] = (mine + outer_in[i].astype(jnp.float32)).astype(jnp.bfloat16)
            cross(i).start()

            @pl.when(i > 0)
            def _():
                finish(i - 1)

    def error_copy(n):
        src, spot = (gap_half, keep) if n == 0 else (gap, give)
        return remote(src.at[1 - r], err_ref.at[:, spot], v_s.at[n], v_r.at[n], sib)

    pl.loop(0, n_f)(chunk)
    for step in range(2):
        b = r if step == 0 else 1 - r
        gap_copies[step].wait_recv()
        sc = jnp.concatenate([sp[step, :, 0:128]] * (half // 128), axis=1)
        cot[b] = (gap[b].astype(jnp.float32) * sc * norm).astype(jnp.bfloat16)

    @pl.when(r == x)
    def _():
        error_copy(0).start()
        error_copy(1).start()
        err_ref[:, keep] = gap_half[r]
        err_ref[:, give] = gap[r]

    pl.loop(n_f, n_c)(chunk)

    @pl.when(outer)
    def _():
        @pl.loop(0, n_c)
        def _(i):
            down(i).wait_recv()
            up(i).wait_send()

    @pl.when(jnp.logical_not(outer))
    def _():
        finish(n_c - 1)

        @pl.loop(0, n_c)
        def _(i):
            cross(i).wait_send()
            down(i).wait_send()

    @pl.when(r == x)
    def _():
        error_copy(0).wait_send()
        error_copy(1).wait_send()

    @pl.when(r != x)
    def _():
        error_copy(0).wait_recv()
        error_copy(1).wait_recv()

    for c in [sib_t, sib_o, sib_x] + z_copies + gap_copies:
        c.wait_send()
    for pair in t_copies + s_copies:
        for c in pair:
            c.wait_send()


def shards_fused(
    teacher_rows, teacher_gain, teacher_value, student_rows, student_gain, student_value, owners
):
    blk, tk = teacher_rows.shape
    slots, sk = student_rows.shape
    cols = teacher_value.shape[1]
    half = cols // 2
    n_mp = lax.axis_size("mp")
    cap = slots // (2 * n_mp)
    wide = -(-blk // 128) * 128
    own = jnp.pad(owners[:, 0], (0, wide - blk), constant_values=-1)
    own = jnp.broadcast_to(own[None, :], (8, wide))
    n_c = 2 * (sk // 256)
    bf, f32, vmem, dma = jnp.bfloat16, jnp.float32, pltpu.VMEM, pltpu.SemaphoreType.DMA
    hbm = pl.BlockSpec(memory_space=pl.ANY)
    inv = pl.BlockSpec(memory_space=vmem)
    scratch = [
        vmem((2, blk, tk), bf),
        vmem((2, slots, sk), bf),
        vmem((tk, cols), bf),
        vmem((sk, cols), bf),
        vmem((2, 8, wide), jnp.int32),
        vmem((blk, 512), bf),
        vmem((2, blk, cols), f32),
        vmem((2, slots, cols), f32),
        vmem((wide, 128), f32),
        vmem((slots, 128), f32),
        vmem((2, blk, half), bf),
        vmem((2, blk, half), bf),
        vmem((2, slots, half), bf),
        vmem((2, slots, half), bf),
        vmem((2, 8, wide), f32),
        vmem((2, 8, wide), f32),
        vmem((2, 8, slots), f32),
        vmem((2, 8, slots), f32),
        vmem((2 * n_mp, 2, cap, half), bf),
        vmem((2, n_mp, 2, cap, half), bf),
        vmem((2, slots, half), bf),
        vmem((2, slots, half), bf),
        vmem((2, slots, half), bf),
        vmem((n_c, 256, half), bf),
        vmem((n_c, 256, half), bf),
        vmem((n_c, 256, half), bf),
        dma((5,)),
        dma((3,)), dma((3,)),
        dma((4,)), dma((4,)),
        dma((4,)), dma((4,)),
        dma((3,)), dma((3,)),
        dma((2,)), dma((2,)),
        dma((2,)), dma((2,)),
        dma((n_c,)), dma((n_c,)),
        dma((n_c,)), dma((n_c,)),
        dma((n_c,)), dma((n_c,)),
    ]
    err, grad = pl.pallas_call(
        fused,
        out_shape=(
            jax.ShapeDtypeStruct((slots, cols), bf),
            jax.ShapeDtypeStruct((sk, cols), bf),
        ),
        in_specs=[hbm, inv, hbm, hbm, inv, hbm, hbm],
        out_specs=(inv, inv),
        scratch_shapes=scratch,
        compiler_params=pltpu.CompilerParams(
            collective_id=1, has_side_effects=True, vmem_limit_bytes=58 * 2**20
        ),
        cost_estimate=pl.CostEstimate(
            flops=10 * 10**9, bytes_accessed=20 * 10**6, transcendentals=0
        ),
    )(
        teacher_rows, teacher_gain[None, :], teacher_value,
        student_rows, student_gain[None, :], student_value, own,
    )
    return err, grad.astype(f32)


def solution(mesh):
    sizes = (mesh.shape["mp"], mesh.shape["role"], mesh.shape["rep"])
    return jax.shard_map(
        shards_fused if sizes == (4, 2, 2) else shards,
        mesh=mesh,
        in_specs=(
            P(("groups", "mp", "role"), "rep"),
            P("rep"),
            P("rep", "role"),
            P(("groups", "mp", "role"), "rep"),
            P("rep"),
            P("rep", "role"),
            P(("groups", "mp", "role"), None),
        ),
        out_specs=(P(("groups", "mp", "role"), "rep"), P(("groups", "rep"), "role")),
        check_vma=False,
    )
```

```python
import math

import jax
import jax.numpy as jnp
from jax import lax
from jax.experimental import pallas as pl
from jax.experimental.pallas import tpu as pltpu
from jax.sharding import PartitionSpec as P

DT = 8192
DS = 5120
KV = 1024


EPS = 1e-06


def squares_of(rows_in):
    widened = rows_in.astype(jnp.float32)
    return jnp.sum(widened * widened, axis=1)


def shards(
    teacher_rows, teacher_gain, teacher_value, student_rows, student_gain, student_value, owners
):
    peer_count = lax.axis_size(("mp", "role"))
    block_rows = teacher_rows.shape[0]
    slot_cap = student_rows.shape[0] // peer_count
    teacher_full, student_full = (
        lax.all_gather(teacher_value, "role", axis=1, tiled=True),
        lax.all_gather(student_value, "role", axis=1, tiled=True),
    )
    teacher_gated = (teacher_rows.astype(jnp.float32) * teacher_gain[None, :]).astype(jnp.bfloat16)
    student_gated = (student_rows.astype(jnp.float32) * student_gain[None, :]).astype(jnp.bfloat16)
    teacher_squares, student_squares = lax.psum(
        (squares_of(teacher_rows), squares_of(student_rows)), "rep"
    )
    teacher_scale = lax.rsqrt(teacher_squares / DT + EPS)
    student_scale = lax.rsqrt(student_squares / DS + EPS)
    teacher_part = jnp.dot(teacher_gated, teacher_full, preferred_element_type=jnp.float32)
    student_part = jnp.dot(student_gated, student_full, preferred_element_type=jnp.float32)
    teacher_sum, student_sum = (
        lax.psum_scatter(teacher_part, "rep", scatter_dimension=1, tiled=True),
        lax.psum_scatter(student_part, "rep", scatter_dimension=1, tiled=True),
    )
    teacher_values = (teacher_sum * teacher_scale[:, None]).astype(jnp.bfloat16)
    student_values = student_sum * student_scale[:, None]
    owner_col = owners[:, 0]
    all_owners = lax.all_gather(owner_col, ("mp", "role"), axis=0, tiled=True).reshape(
        peer_count, block_rows
    )
    myself = lax.axis_index(("mp", "role"))
    is_mine = (all_owners == myself).astype(jnp.int32)
    counts = jnp.sum(is_mine, axis=1)
    live_slot = (jnp.arange(slot_cap, dtype=jnp.int32)[None, :] < counts[:, None]).reshape(-1)
    every_row = lax.all_gather(teacher_values, ("mp", "role"), axis=0, tiled=True)
    rank_in = jnp.cumsum(is_mine, axis=1) - is_mine
    blocks = jnp.arange(peer_count, dtype=jnp.int32)[:, None]
    where_to = jnp.where(is_mine > 0, blocks * slot_cap + rank_in, peer_count * slot_cap)
    source = blocks * block_rows + jnp.arange(block_rows, dtype=jnp.int32)[None, :]
    pick_rows = (
        jnp.zeros((peer_count * slot_cap,), jnp.int32)
        .at[where_to.reshape(-1)]
        .set(source.reshape(-1), mode="drop")
    )
    target = jnp.take(every_row, pick_rows, axis=0)
    value_gap = jnp.where(live_slot[:, None], student_values - target.astype(jnp.float32), 0.0)
    value_error = value_gap.astype(jnp.bfloat16)
    tokens = peer_count * block_rows
    cotangent = (value_gap * student_scale[:, None] * (1.0 / math.sqrt(tokens))).astype(
        jnp.bfloat16
    )
    cotangent_full = lax.all_gather(cotangent, "rep", axis=1, tiled=True)
    half_cols = KV // lax.axis_size("role")
    role_index = lax.axis_index("role")
    grad_part = lax.dot_general(
        student_gated, cotangent_full, (((0,), (0,)), ((), ())), preferred_element_type=jnp.float32
    )
    grad_total = lax.psum(grad_part.astype(jnp.bfloat16), ("mp", "role")).astype(jnp.float32)
    grad_value = lax.dynamic_slice_in_dim(grad_total, role_index * half_cols, half_cols, 1)
    return (value_error, grad_value)


MESH = pl.DeviceIdType.MESH
SENTINEL = 1048576.0


def fused(
    t_hbm, tg_ref, tw_hbm, s_hbm, sg_ref, sw_hbm, ow_ref,
    err_ref, grad_ref,
    tr, sr, tw, sw, ow, srt, tp, sp, tsq, ssq, tx_out, tx_in, sx_out, sx_in,
    tq_out, tq_in, sq_out, sq_in, pk, tgt, gap, gap_half, cot, sc_ref, part_out, outer_in, mid_in,
    lsem, sib_s, sib_r, x_s, x_r, q_s, q_r, z_s, z_r, g_s, g_r, v_s, v_r,
    a_s, a_r, b_s, b_r, c_s, c_r,
):
    g, m = lax.axis_index("groups"), lax.axis_index("mp")
    r, x = lax.axis_index("role"), lax.axis_index("rep")
    blk, tk = t_hbm.shape
    slots, sk = s_hbm.shape
    cols = tw_hbm.shape[1]
    half = cols // 2
    n_mp = lax.axis_size("mp")
    cap = slots // (2 * n_mp)
    tokens = blk * 2 * n_mp
    fb = 256
    n_f = sk // fb
    sib = (g, m, 1 - r, x)
    xp = (g, m, r, 1 - x)

    def z_dev(k):
        return (g, lax.rem(m + k, n_mp), r, x)

    peers = [sib, xp] + [z_dev(k) for k in range(1, n_mp)]
    barrier = pltpu.get_barrier_semaphore()
    for d in peers:
        pl.semaphore_signal(barrier, inc=1, device_id=d, device_id_type=MESH)

    loc = [
        pltpu.make_async_copy(t_hbm, tr.at[r], lsem.at[0]),
        pltpu.make_async_copy(tw_hbm, tw, lsem.at[1]),
        pltpu.make_async_copy(s_hbm, sr.at[r], lsem.at[2]),
        pltpu.make_async_copy(sw_hbm, sw, lsem.at[3]),
    ]
    for n in (0, 1):
        loc[n].start()
    wide = ow.shape[2]
    ow[r] = jnp.full((8, wide), -1.0, jnp.float32)
    ow[r, :, 0:blk] = jnp.broadcast_to(ow_ref[...].astype(jnp.float32), (8, blk))
    pl.semaphore_wait(barrier, len(peers))

    def remote(src, dst, ss, rs, dev):
        return pltpu.make_async_remote_copy(
            src_ref=src, dst_ref=dst, send_sem=ss, recv_sem=rs, device_id=dev, device_id_type=MESH
        )

    sib_t = remote(t_hbm, tr.at[r], sib_s.at[0], sib_r.at[0], sib)
    sib_o = remote(ow.at[r], ow.at[r], sib_s.at[1], sib_r.at[1], sib)
    sib_x = remote(s_hbm, sr.at[r], sib_s.at[2], sib_r.at[2], sib)
    sib_t.start()
    sib_o.start()

    keep = pl.ds(pl.multiple_of(x * half, half), half)
    give = pl.ds(pl.multiple_of((1 - x) * half, half), half)

    ones = jnp.ones((512, 128), jnp.bfloat16)

    def project(src, b, in_place, out, gain, w, sq):
        kt = ones.shape[0]
        sq[...] = jnp.zeros_like(sq)
        out[...] = jnp.zeros_like(out)
        rows = src.shape[1]

        @pl.loop(0, src.shape[2] // kt)
        def _(k):
            ks = pl.ds(pl.multiple_of(k * kt, kt), kt)
            v = src[b, :, ks].astype(jnp.float32)
            lanes = [gain[pl.ds(k * (kt // 128) + j, 1), :] for j in range(kt // 128)]
            gated = (v * jnp.concatenate(lanes, axis=1)).astype(jnp.bfloat16)
            if in_place:
                src[b, :, ks] = gated
            out[...] += jnp.dot(gated, w[ks, :], preferred_element_type=jnp.float32)
            sq[0:rows, :] += jnp.dot(
                (v * v).astype(jnp.bfloat16), ones, preferred_element_type=jnp.float32
            )

    def stage(out, stage_out, sq, q_out, slot):
        stage_out[slot] = out[:, give].astype(jnp.bfloat16)
        q_out[slot] = jnp.broadcast_to(
            sq[...].T[0:1], q_out.shape[1:]
        )

    def x_pair(stage_out, stage_in, q_out, q_in, slot, n):
        return (
            remote(stage_out.at[slot], stage_in.at[slot], x_s.at[n], x_r.at[n], xp),
            remote(q_out.at[slot], q_in.at[slot], q_s.at[n], q_r.at[n], xp),
        )

    t_copies = []
    for step in range(2):
        b = r if step == 0 else 1 - r
        if step == 0:
            loc[0].wait()
            loc[1].wait()
            loc[2].start()
            loc[3].start()
            sib_x.start()
        else:
            sib_t.wait_recv()
        project(tr, b, False, tp.at[step], tg_ref, tw, tsq)
        stage(tp.at[step], tx_out, tsq, tq_out, step)
        pair = x_pair(tx_out, tx_in, tq_out, tq_in, step, step)
        for c in pair:
            c.start()
        t_copies.append(pair)

    s_copies = []

    def student(step):
        b = r if step == 0 else 1 - r
        if step == 0:
            loc[2].wait()
            loc[3].wait()
        else:
            sib_x.wait_recv()
        project(sr, b, True, sp.at[step], sg_ref, sw, ssq)
        for sub in range(2):
            spot = pl.ds(pl.multiple_of((1 - x) * half + sub * 128, 128), 128)
            sx_out[step, sub] = sp[step, :, spot].astype(jnp.bfloat16)
        sq_out[step] = jnp.broadcast_to(ssq[...].T[0:1], sq_out.shape[1:])
        q = remote(sq_out.at[step], sq_in.at[step], q_s.at[2 + step], q_r.at[2 + step], xp)
        subs = [
            remote(
                sx_out.at[step, sub], sx_in.at[step, sub],
                x_s.at[2 + 2 * step + sub], x_r.at[2 + 2 * step + sub], xp,
            )
            for sub in range(2)
        ]
        for c in [q] + subs:
            c.start()
        s_copies.append([q] + subs)

        @pl.loop(0, n_f)
        def _(f):
            fs = pl.ds(pl.multiple_of(f * fb, fb), fb)
            srt[b, fs, :] = sr[b, :, fs].T

    def column(row):
        n = row.shape[1]
        return jnp.broadcast_to(row, (128, n)).T

    sib_o.wait_recv()
    n_own = 2 * n_mp
    z_copies = []
    for step in range(2):
        for c in t_copies[step]:
            c.wait_recv()
        b = r if step == 0 else 1 - r
        sq_sum = tq_out[step, 0:1, :] + tq_in[step, 0:1, :]
        scale = column(lax.rsqrt(sq_sum / DT + EPS))[0:blk]
        scale = jnp.concatenate([scale] * (half // 128), axis=1)
        values = tp[step, :, keep] + tx_in[step].astype(jnp.float32)
        values = (values * scale).astype(jnp.bfloat16)
        own = ow[b]
        row_id = lax.broadcasted_iota(jnp.int32, (8, wide), 0).astype(jnp.float32)
        eq = (own == row_id).astype(jnp.float32)
        upper = (
            lax.broadcasted_iota(jnp.int32, (wide, wide), 0)
            < lax.broadcasted_iota(jnp.int32, (wide, wide), 1)
        ).astype(jnp.float32)
        before = jnp.dot(
            eq.astype(jnp.bfloat16), upper.astype(jnp.bfloat16), preferred_element_type=jnp.float32
        )
        rank = jnp.sum(eq * before, axis=0, keepdims=True)
        dest = own[0:1, :] * cap + rank
        for o in range(n_own // 2):
            spot = lax.broadcasted_iota(jnp.int32, (2 * cap, wide), 0) + o * 2 * cap
            hit = (spot.astype(jnp.float32) == dest).astype(jnp.float32)
            filled = jnp.sum(hit, axis=1, keepdims=True)
            moved = jnp.dot(
                hit[:, 0:blk].astype(jnp.bfloat16), values, preferred_element_type=jnp.float32
            )
            moved = jnp.where(filled > 0.5, moved, SENTINEL).astype(jnp.bfloat16)
            pk[2 * o, b] = moved[0:cap]
            pk[2 * o + 1, b] = moved[cap:]
        for k in range(1, n_mp):
            to = lax.rem(m + k, n_mp)
            n = step * (n_mp - 1) + k - 1
            c = remote(
                pk.at[pl.ds(2 * to, 2), b], tgt.at[:, m, b], z_s.at[n], z_r.at[n], z_dev(k)
            )
            c.start()
            z_copies.append(c)
        tgt[0, m, b] = pk[2 * m, b]
        tgt[1, m, b] = pk[2 * m + 1, b]
        if step == 0:
            student(0)

    student(1)
    for c in z_copies:
        c.wait_recv()

    norm = 1.0 / math.sqrt(tokens)
    gap_copies = []

    def close_gap(sub):
        spot = pl.ds(pl.multiple_of(x * half + sub * 128, 128), 128)
        for step in range(2):
            b = r if step == 0 else 1 - r
            s_copies[step][1 + sub].wait_recv()
            if sub == 0:
                s_copies[step][0].wait_recv()
                sq_sum = sq_out[step, 0:1, :] + sq_in[step, 0:1, :]
                sc_ref[b] = column(lax.rsqrt(sq_sum / DS + EPS))
            per = 2 * cap
            for k in range(n_mp):
                rs = slice(k * per, (k + 1) * per)
                sc = sc_ref[b, rs]
                vals = (sp[step, rs, spot] + sx_in[step, sub, rs].astype(jnp.float32)) * sc
                target = tgt[b, k, :, :, sub * 128 : sub * 128 + 128].reshape(per, 128)
                target = target.astype(jnp.float32)
                diff = jnp.where(target < 0.5 * SENTINEL, vals - target, 0.0)
                gap_half[sub, b, rs] = diff.astype(jnp.bfloat16)
                cot[sub, b, rs] = (diff * sc * norm).astype(jnp.bfloat16)
            n = 2 * sub + step
            c = remote(gap_half.at[sub, b], gap.at[sub, b], g_s.at[n], g_r.at[n], xp)
            c.start()
            gap_copies.append(c)

    outer = (m == 0) | (m == n_mp - 1)
    inward = jnp.where(m < n_mp // 2, m + 1, m - 1)
    outward = jnp.where(m < n_mp // 2, m - 1, m + 1)
    near = (g, jnp.where(outer, inward, outward), r, x)
    across = (g, inward, r, x)
    n_c = 4 * n_f
    lag = 3

    def up(i):
        return remote(part_out.at[i], outer_in.at[i], a_s.at[i], a_r.at[i], near)

    def cross(i):
        return remote(part_out.at[i], mid_in.at[i], b_s.at[i], b_r.at[i], across)

    def place(i):
        f = lax.rem(i, n_f)
        phase = i // n_f
        h = jnp.where(phase < 2, x, 1 - x)
        return (
            pl.ds(pl.multiple_of(f * fb, fb), fb),
            pl.ds(pl.multiple_of(h * half + lax.rem(phase, 2) * 128, 128), 128),
        )

    def down(i):
        spot = grad_ref.at[place(i)]
        return remote(spot, spot, c_s.at[i], c_r.at[i], near)

    def grad_part(i):
        f = lax.rem(i, n_f)
        fs = pl.ds(pl.multiple_of(f * fb, fb), fb)
        total = None
        for b in range(2):
            term = jnp.dot(srt[b, fs, :], cot[i // n_f, b], preferred_element_type=jnp.float32)
            total = term if total is None else total + term
        return total

    def finish(i):
        cross(i).wait_recv()
        both = part_out[i].astype(jnp.float32) + mid_in[i].astype(jnp.float32)
        grad_ref[place(i)] = both.astype(jnp.bfloat16)
        down(i).start()

    def chunk(i):
        mine = grad_part(i)

        @pl.when(outer)
        def _():
            part_out[i] = mine.astype(jnp.bfloat16)
            up(i).start()

        @pl.when(jnp.logical_not(outer))
        def _():
            up(i).wait_recv()
            part_out[i] = (mine + outer_in[i].astype(jnp.float32)).astype(jnp.bfloat16)
            cross(i).start()

            @pl.when(i >= lag)
            def _():
                finish(i - lag)

    def error_spot(n):
        h = x if n < 2 else 1 - x
        return pl.ds(pl.multiple_of(h * half + (n % 2) * 128, 128), 128)

    def error_from(n, b):
        return (gap_half if n < 2 else gap).at[n % 2, b]

    def error_copy(n):
        return remote(
            error_from(n, 1 - r), err_ref.at[:, error_spot(n)], v_s.at[n], v_r.at[n], sib
        )

    close_gap(0)
    pl.loop(0, 4)(chunk)
    close_gap(1)
    pl.loop(4, 2 * n_f)(chunk)
    for c in gap_copies:
        c.wait_recv()
    for sub in range(2):
        for b in range(2):
            cot[2 + sub, b] = (
                gap[sub, b].astype(jnp.float32) * sc_ref[b] * norm
            ).astype(jnp.bfloat16)

    @pl.when(r == x)
    def _():
        for n in range(4):
            error_copy(n).start()
            err_ref[:, error_spot(n)] = error_from(n, r)[...]

    pl.loop(2 * n_f, n_c)(chunk)

    @pl.when(outer)
    def _():
        @pl.loop(0, n_c)
        def _(i):
            down(i).wait_recv()
            up(i).wait_send()

    @pl.when(jnp.logical_not(outer))
    def _():
        pl.loop(n_c - lag, n_c)(finish)

        @pl.loop(0, n_c)
        def _(i):
            cross(i).wait_send()
            down(i).wait_send()

    @pl.when(r == x)
    def _():
        for n in range(4):
            error_copy(n).wait_send()

    @pl.when(r != x)
    def _():
        for n in range(4):
            error_copy(n).wait_recv()

    for c in [sib_t, sib_o, sib_x] + z_copies + gap_copies:
        c.wait_send()
    for pair in t_copies + s_copies:
        for c in pair:
            c.wait_send()


def shards_fused(
    teacher_rows, teacher_gain, teacher_value, student_rows, student_gain, student_value, owners
):
    blk, tk = teacher_rows.shape
    slots, sk = student_rows.shape
    cols = teacher_value.shape[1]
    half = cols // 2
    n_mp = lax.axis_size("mp")
    cap = slots // (2 * n_mp)
    wide = -(-blk // 128) * 128
    n_c = 4 * (sk // 256)
    bf, f32, vmem, dma = jnp.bfloat16, jnp.float32, pltpu.VMEM, pltpu.SemaphoreType.DMA
    hbm = pl.BlockSpec(memory_space=pl.ANY)
    inv = pl.BlockSpec(memory_space=vmem)
    scratch = [
        vmem((2, blk, tk), bf),
        vmem((2, slots, sk), bf),
        vmem((tk, cols), bf),
        vmem((sk, cols), bf),
        vmem((2, 8, wide), f32),
        vmem((2, sk, slots), bf),
        vmem((2, blk, cols), f32),
        vmem((2, slots, cols), f32),
        vmem((wide, 128), f32),
        vmem((slots, 128), f32),
        vmem((2, blk, half), bf),
        vmem((2, blk, half), bf),
        vmem((2, 2, slots, 128), bf),
        vmem((2, 2, slots, 128), bf),
        vmem((2, 8, wide), f32),
        vmem((2, 8, wide), f32),
        vmem((2, 8, slots), f32),
        vmem((2, 8, slots), f32),
        vmem((2 * n_mp, 2, cap, half), bf),
        vmem((2, n_mp, 2, cap, half), bf),
        vmem((2, 2, slots, 128), bf),
        vmem((2, 2, slots, 128), bf),
        vmem((4, 2, slots, 128), bf),
        vmem((2, slots, 128), f32),
        vmem((n_c, 256, 128), bf),
        vmem((n_c, 256, 128), bf),
        vmem((n_c, 256, 128), bf),
        dma((4,)),
        dma((3,)), dma((3,)),
        dma((6,)), dma((6,)),
        dma((4,)), dma((4,)),
        dma((2 * n_mp - 2,)), dma((2 * n_mp - 2,)),
        dma((4,)), dma((4,)),
        dma((4,)), dma((4,)),
        dma((n_c,)), dma((n_c,)),
        dma((n_c,)), dma((n_c,)),
        dma((n_c,)), dma((n_c,)),
    ]
    err, grad = pl.pallas_call(
        fused,
        out_shape=(
            jax.ShapeDtypeStruct((slots, cols), bf),
            jax.ShapeDtypeStruct((sk, cols), bf),
        ),
        in_specs=[hbm, inv, hbm, hbm, inv, hbm, inv],
        out_specs=(inv, inv),
        scratch_shapes=scratch,
        compiler_params=pltpu.CompilerParams(
            collective_id=1, has_side_effects=True, vmem_limit_bytes=58 * 2**20
        ),
        cost_estimate=pl.CostEstimate(
            flops=10 * 10**9, bytes_accessed=20 * 10**6, transcendentals=0
        ),
    )(
        teacher_rows, teacher_gain.reshape(-1, 128), teacher_value,
        student_rows, student_gain.reshape(-1, 128), student_value, owners.reshape(1, blk),
    )
    return err, grad.astype(f32)


def solution(mesh):
    sizes = (mesh.shape["mp"], mesh.shape["role"], mesh.shape["rep"])
    return jax.shard_map(
        shards_fused if sizes == (4, 2, 2) else shards,
        mesh=mesh,
        in_specs=(
            P(("groups", "mp", "role"), "rep"),
            P("rep"),
            P("rep", "role"),
            P(("groups", "mp", "role"), "rep"),
            P("rep"),
            P("rep", "role"),
            P(("groups", "mp", "role"), None),
        ),
        out_specs=(P(("groups", "mp", "role"), "rep"), P(("groups", "rep"), "role")),
        check_vma=False,
    )
```

```python
import math

import jax
import jax.numpy as jnp
from jax import lax
from jax.experimental import pallas as pl
from jax.experimental.pallas import tpu as pltpu
from jax.sharding import PartitionSpec as P

DT = 8192
DS = 5120
KV = 1024


EPS = 1e-06


def squares_of(rows_in):
    widened = rows_in.astype(jnp.float32)
    return jnp.sum(widened * widened, axis=1)


def shards(
    teacher_rows, teacher_gain, teacher_value, student_rows, student_gain, student_value, owners
):
    peer_count = lax.axis_size(("mp", "role"))
    block_rows = teacher_rows.shape[0]
    slot_cap = student_rows.shape[0] // peer_count
    teacher_full, student_full = (
        lax.all_gather(teacher_value, "role", axis=1, tiled=True),
        lax.all_gather(student_value, "role", axis=1, tiled=True),
    )
    teacher_gated = (teacher_rows.astype(jnp.float32) * teacher_gain[None, :]).astype(jnp.bfloat16)
    student_gated = (student_rows.astype(jnp.float32) * student_gain[None, :]).astype(jnp.bfloat16)
    teacher_squares, student_squares = lax.psum(
        (squares_of(teacher_rows), squares_of(student_rows)), "rep"
    )
    teacher_scale = lax.rsqrt(teacher_squares / DT + EPS)
    student_scale = lax.rsqrt(student_squares / DS + EPS)
    teacher_part = jnp.dot(teacher_gated, teacher_full, preferred_element_type=jnp.float32)
    student_part = jnp.dot(student_gated, student_full, preferred_element_type=jnp.float32)
    teacher_sum, student_sum = (
        lax.psum_scatter(teacher_part, "rep", scatter_dimension=1, tiled=True),
        lax.psum_scatter(student_part, "rep", scatter_dimension=1, tiled=True),
    )
    teacher_values = (teacher_sum * teacher_scale[:, None]).astype(jnp.bfloat16)
    student_values = student_sum * student_scale[:, None]
    owner_col = owners[:, 0]
    all_owners = lax.all_gather(owner_col, ("mp", "role"), axis=0, tiled=True).reshape(
        peer_count, block_rows
    )
    myself = lax.axis_index(("mp", "role"))
    is_mine = (all_owners == myself).astype(jnp.int32)
    counts = jnp.sum(is_mine, axis=1)
    live_slot = (jnp.arange(slot_cap, dtype=jnp.int32)[None, :] < counts[:, None]).reshape(-1)
    every_row = lax.all_gather(teacher_values, ("mp", "role"), axis=0, tiled=True)
    rank_in = jnp.cumsum(is_mine, axis=1) - is_mine
    blocks = jnp.arange(peer_count, dtype=jnp.int32)[:, None]
    where_to = jnp.where(is_mine > 0, blocks * slot_cap + rank_in, peer_count * slot_cap)
    source = blocks * block_rows + jnp.arange(block_rows, dtype=jnp.int32)[None, :]
    pick_rows = (
        jnp.zeros((peer_count * slot_cap,), jnp.int32)
        .at[where_to.reshape(-1)]
        .set(source.reshape(-1), mode="drop")
    )
    target = jnp.take(every_row, pick_rows, axis=0)
    value_gap = jnp.where(live_slot[:, None], student_values - target.astype(jnp.float32), 0.0)
    value_error = value_gap.astype(jnp.bfloat16)
    tokens = peer_count * block_rows
    cotangent = (value_gap * student_scale[:, None] * (1.0 / math.sqrt(tokens))).astype(
        jnp.bfloat16
    )
    cotangent_full = lax.all_gather(cotangent, "rep", axis=1, tiled=True)
    half_cols = KV // lax.axis_size("role")
    role_index = lax.axis_index("role")
    grad_part = lax.dot_general(
        student_gated, cotangent_full, (((0,), (0,)), ((), ())), preferred_element_type=jnp.float32
    )
    grad_total = lax.psum(grad_part.astype(jnp.bfloat16), ("mp", "role")).astype(jnp.float32)
    grad_value = lax.dynamic_slice_in_dim(grad_total, role_index * half_cols, half_cols, 1)
    return (value_error, grad_value)


MESH = pl.DeviceIdType.MESH
SENTINEL = 1048576.0


def fused(
    t_hbm, tg_ref, tw_hbm, s_hbm, sg_ref, sw_hbm, ow_ref,
    err_ref, grad_ref,
    tr, sr, tw, sw, ow, srt, tp, sp, tsq, ssq, tx_out, tx_in, sx_out, sx_in,
    tq_out, tq_in, sq_out, sq_in, pk, tgt, gap, gap_half, cot, sc_ref, part_out, outer_in, mid_in,
    lsem, sib_s, sib_r, x_s, x_r, q_s, q_r, z_s, z_r, g_s, g_r, v_s, v_r,
    a_s, a_r, b_s, b_r, c_s, c_r,
):
    g, m = lax.axis_index("groups"), lax.axis_index("mp")
    r, x = lax.axis_index("role"), lax.axis_index("rep")
    blk, tk = t_hbm.shape
    slots, sk = s_hbm.shape
    cols = tw_hbm.shape[1]
    half = cols // 2
    n_mp = lax.axis_size("mp")
    cap = slots // (2 * n_mp)
    tokens = blk * 2 * n_mp
    fb = 256
    n_f = sk // fb
    sib = (g, m, 1 - r, x)
    xp = (g, m, r, 1 - x)

    def z_dev(k):
        return (g, lax.rem(m + k, n_mp), r, x)

    peers = [sib, xp] + [z_dev(k) for k in range(1, n_mp)]
    barrier = pltpu.get_barrier_semaphore()
    for d in peers:
        pl.semaphore_signal(barrier, inc=1, device_id=d, device_id_type=MESH)

    loc = [
        pltpu.make_async_copy(t_hbm, tr.at[r], lsem.at[0]),
        pltpu.make_async_copy(tw_hbm, tw, lsem.at[1]),
        pltpu.make_async_copy(s_hbm, sr.at[r], lsem.at[2]),
        pltpu.make_async_copy(sw_hbm, sw, lsem.at[3]),
    ]
    for n in (0, 1):
        loc[n].start()
    wide = ow.shape[2]
    ow[r] = jnp.full((8, wide), -1.0, jnp.float32)
    ow[r, :, 0:blk] = jnp.broadcast_to(ow_ref[...].astype(jnp.float32), (8, blk))
    pl.semaphore_wait(barrier, len(peers))

    def remote(src, dst, ss, rs, dev):
        return pltpu.make_async_remote_copy(
            src_ref=src, dst_ref=dst, send_sem=ss, recv_sem=rs, device_id=dev, device_id_type=MESH
        )

    sib_t = remote(t_hbm, tr.at[r], sib_s.at[0], sib_r.at[0], sib)
    sib_o = remote(ow.at[r], ow.at[r], sib_s.at[1], sib_r.at[1], sib)
    sib_x = remote(s_hbm, sr.at[r], sib_s.at[2], sib_r.at[2], sib)
    sib_t.start()
    sib_o.start()

    keep = pl.ds(pl.multiple_of(x * half, half), half)
    give = pl.ds(pl.multiple_of((1 - x) * half, half), half)

    ones = jnp.ones((512, 128), jnp.bfloat16)

    def project(src, b, in_place, out, gain, w, sq):
        kt = ones.shape[0]
        sq[...] = jnp.zeros_like(sq)
        out[...] = jnp.zeros_like(out)
        rows = src.shape[1]

        @pl.loop(0, src.shape[2] // kt)
        def _(k):
            ks = pl.ds(pl.multiple_of(k * kt, kt), kt)
            v = src[b, :, ks].astype(jnp.float32)
            lanes = [gain[pl.ds(k * (kt // 128) + j, 1), :] for j in range(kt // 128)]
            gated = (v * jnp.concatenate(lanes, axis=1)).astype(jnp.bfloat16)
            if in_place:
                src[b, :, ks] = gated
            out[...] += jnp.dot(gated, w[ks, :], preferred_element_type=jnp.float32)
            sq[0:rows, :] += jnp.dot(
                (v * v).astype(jnp.bfloat16), ones, preferred_element_type=jnp.float32
            )

    def stage(out, stage_out, sq, q_out, slot):
        stage_out[slot] = out[:, give].astype(jnp.bfloat16)
        q_out[slot] = jnp.broadcast_to(
            sq[...].T[0:1], q_out.shape[1:]
        )

    def x_pair(stage_out, stage_in, q_out, q_in, slot, n):
        return (
            remote(stage_out.at[slot], stage_in.at[slot], x_s.at[n], x_r.at[n], xp),
            remote(q_out.at[slot], q_in.at[slot], q_s.at[n], q_r.at[n], xp),
        )

    t_copies = []
    for step in range(2):
        b = r if step == 0 else 1 - r
        if step == 0:
            loc[0].wait()
            loc[1].wait()
            loc[2].start()
            loc[3].start()
            sib_x.start()
        else:
            sib_t.wait_recv()
        project(tr, b, False, tp.at[step], tg_ref, tw, tsq)
        stage(tp.at[step], tx_out, tsq, tq_out, step)
        pair = x_pair(tx_out, tx_in, tq_out, tq_in, step, step)
        for c in pair:
            c.start()
        t_copies.append(pair)

    s_copies = []

    def student(step):
        b = r if step == 0 else 1 - r
        if step == 0:
            loc[2].wait()
            loc[3].wait()
        else:
            sib_x.wait_recv()
        project(sr, b, True, sp.at[step], sg_ref, sw, ssq)
        for sub in range(2):
            spot = pl.ds(pl.multiple_of((1 - x) * half + sub * 128, 128), 128)
            sx_out[step, sub] = sp[step, :, spot].astype(jnp.bfloat16)
        sq_out[step] = jnp.broadcast_to(ssq[...].T[0:1], sq_out.shape[1:])
        q = remote(sq_out.at[step], sq_in.at[step], q_s.at[2 + step], q_r.at[2 + step], xp)
        subs = [
            remote(
                sx_out.at[step, sub], sx_in.at[step, sub],
                x_s.at[2 + 2 * step + sub], x_r.at[2 + 2 * step + sub], xp,
            )
            for sub in range(2)
        ]
        for c in [q] + subs:
            c.start()
        s_copies.append([q] + subs)

    def column(row):
        n = row.shape[1]
        return jnp.broadcast_to(row, (128, n)).T

    sib_o.wait_recv()
    n_own = 2 * n_mp
    z_copies = []
    for step in range(2):
        for c in t_copies[step]:
            c.wait_recv()
        b = r if step == 0 else 1 - r
        sq_sum = tq_out[step, 0:1, :] + tq_in[step, 0:1, :]
        scale = column(lax.rsqrt(sq_sum / DT + EPS))[0:blk]
        scale = jnp.concatenate([scale] * (half // 128), axis=1)
        values = tp[step, :, keep] + tx_in[step].astype(jnp.float32)
        values = (values * scale).astype(jnp.bfloat16)
        own = ow[b]
        row_id = lax.broadcasted_iota(jnp.int32, (8, wide), 0).astype(jnp.float32)
        eq = (own == row_id).astype(jnp.float32)
        upper = (
            lax.broadcasted_iota(jnp.int32, (wide, wide), 0)
            < lax.broadcasted_iota(jnp.int32, (wide, wide), 1)
        ).astype(jnp.float32)
        before = jnp.dot(
            eq.astype(jnp.bfloat16), upper.astype(jnp.bfloat16), preferred_element_type=jnp.float32
        )
        rank = jnp.sum(eq * before, axis=0, keepdims=True)
        dest = own[0:1, :] * cap + rank
        for o in range(n_own // 2):
            spot = lax.broadcasted_iota(jnp.int32, (2 * cap, wide), 0) + o * 2 * cap
            hit = (spot.astype(jnp.float32) == dest).astype(jnp.float32)
            filled = jnp.sum(hit, axis=1, keepdims=True)
            moved = jnp.dot(
                hit[:, 0:blk].astype(jnp.bfloat16), values, preferred_element_type=jnp.float32
            )
            moved = jnp.where(filled > 0.5, moved, SENTINEL).astype(jnp.bfloat16)
            pk[2 * o, b] = moved[0:cap]
            pk[2 * o + 1, b] = moved[cap:]
        for k in range(1, n_mp):
            to = lax.rem(m + k, n_mp)
            n = step * (n_mp - 1) + k - 1
            c = remote(
                pk.at[pl.ds(2 * to, 2), b], tgt.at[:, m, b], z_s.at[n], z_r.at[n], z_dev(k)
            )
            c.start()
            z_copies.append(c)
        tgt[0, m, b] = pk[2 * m, b]
        tgt[1, m, b] = pk[2 * m + 1, b]
        if step == 0:
            student(0)

    student(1)

    @pl.loop(0, n_f)
    def _(f):
        fs = pl.ds(pl.multiple_of(f * fb, fb), fb)
        for b in range(2):
            srt[b, fs, :] = sr[b, :, fs].T

    for c in z_copies:
        c.wait_recv()

    norm = 1.0 / math.sqrt(tokens)
    gap_copies = []

    def close_gap(sub):
        spot = pl.ds(pl.multiple_of(x * half + sub * 128, 128), 128)
        for step in range(2):
            b = r if step == 0 else 1 - r
            s_copies[step][1 + sub].wait_recv()
            if sub == 0:
                s_copies[step][0].wait_recv()
                sq_sum = sq_out[step, 0:1, :] + sq_in[step, 0:1, :]
                sc_ref[b] = column(lax.rsqrt(sq_sum / DS + EPS))
            per = 2 * cap
            for k in range(n_mp):
                rs = slice(k * per, (k + 1) * per)
                sc = sc_ref[b, rs]
                vals = (sp[step, rs, spot] + sx_in[step, sub, rs].astype(jnp.float32)) * sc
                target = tgt[b, k, :, :, sub * 128 : sub * 128 + 128].reshape(per, 128)
                target = target.astype(jnp.float32)
                diff = jnp.where(target < 0.5 * SENTINEL, vals - target, 0.0)
                gap_half[sub, b, rs] = diff.astype(jnp.bfloat16)
                cot[sub, b, rs] = (diff * sc * norm).astype(jnp.bfloat16)
            n = 2 * sub + step
            c = remote(gap_half.at[sub, b], gap.at[sub, b], g_s.at[n], g_r.at[n], xp)
            c.start()
            gap_copies.append(c)

    outer = (m == 0) | (m == n_mp - 1)
    inward = jnp.where(m < n_mp // 2, m + 1, m - 1)
    outward = jnp.where(m < n_mp // 2, m - 1, m + 1)
    near = (g, jnp.where(outer, inward, outward), r, x)
    across = (g, inward, r, x)
    n_c = 4 * n_f
    lag = 3

    def up(i):
        return remote(part_out.at[i], outer_in.at[i], a_s.at[i], a_r.at[i], near)

    def cross(i):
        return remote(part_out.at[i], mid_in.at[i], b_s.at[i], b_r.at[i], across)

    def place(i):
        f = lax.rem(i, n_f)
        phase = i // n_f
        h = jnp.where(phase < 2, x, 1 - x)
        return (
            pl.ds(pl.multiple_of(f * fb, fb), fb),
            pl.ds(pl.multiple_of(h * half + lax.rem(phase, 2) * 128, 128), 128),
        )

    def down(i):
        spot = grad_ref.at[place(i)]
        return remote(spot, spot, c_s.at[i], c_r.at[i], near)

    def grad_part(i):
        f = lax.rem(i, n_f)
        fs = pl.ds(pl.multiple_of(f * fb, fb), fb)
        total = None
        for b in range(2):
            term = jnp.dot(srt[b, fs, :], cot[i // n_f, b], preferred_element_type=jnp.float32)
            total = term if total is None else total + term
        return total

    def finish(i):
        cross(i).wait_recv()
        both = part_out[i].astype(jnp.float32) + mid_in[i].astype(jnp.float32)
        grad_ref[place(i)] = both.astype(jnp.bfloat16)
        down(i).start()

    def chunk(i):
        mine = grad_part(i)

        @pl.when(outer)
        def _():
            part_out[i] = mine.astype(jnp.bfloat16)
            up(i).start()

        @pl.when(jnp.logical_not(outer))
        def _():
            up(i).wait_recv()
            part_out[i] = (mine + outer_in[i].astype(jnp.float32)).astype(jnp.bfloat16)
            cross(i).start()

            @pl.when(i >= lag)
            def _():
                finish(i - lag)

    def error_spot(n):
        h = x if n < 2 else 1 - x
        return pl.ds(pl.multiple_of(h * half + (n % 2) * 128, 128), 128)

    def error_from(n, b):
        return (gap_half if n < 2 else gap).at[n % 2, b]

    def error_copy(n):
        return remote(
            error_from(n, 1 - r), err_ref.at[:, error_spot(n)], v_s.at[n], v_r.at[n], sib
        )

    close_gap(0)
    pl.loop(0, 4)(chunk)
    close_gap(1)
    pl.loop(4, 2 * n_f)(chunk)
    for c in gap_copies:
        c.wait_recv()
    for sub in range(2):
        for b in range(2):
            cot[2 + sub, b] = (
                gap[sub, b].astype(jnp.float32) * sc_ref[b] * norm
            ).astype(jnp.bfloat16)

    @pl.when(r == x)
    def _():
        for n in range(4):
            error_copy(n).start()
            err_ref[:, error_spot(n)] = error_from(n, r)[...]

    pl.loop(2 * n_f, n_c)(chunk)

    @pl.when(outer)
    def _():
        @pl.loop(0, n_c)
        def _(i):
            down(i).wait_recv()
            up(i).wait_send()

    @pl.when(jnp.logical_not(outer))
    def _():
        pl.loop(n_c - lag, n_c)(finish)

        @pl.loop(0, n_c)
        def _(i):
            cross(i).wait_send()
            down(i).wait_send()

    @pl.when(r == x)
    def _():
        for n in range(4):
            error_copy(n).wait_send()

    @pl.when(r != x)
    def _():
        for n in range(4):
            error_copy(n).wait_recv()

    for c in [sib_t, sib_o, sib_x] + z_copies + gap_copies:
        c.wait_send()
    for pair in t_copies + s_copies:
        for c in pair:
            c.wait_send()


def shards_fused(
    teacher_rows, teacher_gain, teacher_value, student_rows, student_gain, student_value, owners
):
    blk, tk = teacher_rows.shape
    slots, sk = student_rows.shape
    cols = teacher_value.shape[1]
    half = cols // 2
    n_mp = lax.axis_size("mp")
    cap = slots // (2 * n_mp)
    wide = -(-blk // 128) * 128
    n_c = 4 * (sk // 256)
    bf, f32, vmem, dma = jnp.bfloat16, jnp.float32, pltpu.VMEM, pltpu.SemaphoreType.DMA
    hbm = pl.BlockSpec(memory_space=pl.ANY)
    inv = pl.BlockSpec(memory_space=vmem)
    scratch = [
        vmem((2, blk, tk), bf),
        vmem((2, slots, sk), bf),
        vmem((tk, cols), bf),
        vmem((sk, cols), bf),
        vmem((2, 8, wide), f32),
        vmem((2, sk, slots), bf),
        vmem((2, blk, cols), f32),
        vmem((2, slots, cols), f32),
        vmem((wide, 128), f32),
        vmem((slots, 128), f32),
        vmem((2, blk, half), bf),
        vmem((2, blk, half), bf),
        vmem((2, 2, slots, 128), bf),
        vmem((2, 2, slots, 128), bf),
        vmem((2, 8, wide), f32),
        vmem((2, 8, wide), f32),
        vmem((2, 8, slots), f32),
        vmem((2, 8, slots), f32),
        vmem((2 * n_mp, 2, cap, half), bf),
        vmem((2, n_mp, 2, cap, half), bf),
        vmem((2, 2, slots, 128), bf),
        vmem((2, 2, slots, 128), bf),
        vmem((4, 2, slots, 128), bf),
        vmem((2, slots, 128), f32),
        vmem((n_c, 256, 128), bf),
        vmem((n_c, 256, 128), bf),
        vmem((n_c, 256, 128), bf),
        dma((4,)),
        dma((3,)), dma((3,)),
        dma((6,)), dma((6,)),
        dma((4,)), dma((4,)),
        dma((2 * n_mp - 2,)), dma((2 * n_mp - 2,)),
        dma((4,)), dma((4,)),
        dma((4,)), dma((4,)),
        dma((n_c,)), dma((n_c,)),
        dma((n_c,)), dma((n_c,)),
        dma((n_c,)), dma((n_c,)),
    ]
    err, grad = pl.pallas_call(
        fused,
        out_shape=(
            jax.ShapeDtypeStruct((slots, cols), bf),
            jax.ShapeDtypeStruct((sk, cols), bf),
        ),
        in_specs=[hbm, inv, hbm, hbm, inv, hbm, inv],
        out_specs=(inv, inv),
        scratch_shapes=scratch,
        compiler_params=pltpu.CompilerParams(
            collective_id=1, has_side_effects=True, vmem_limit_bytes=58 * 2**20
        ),
        cost_estimate=pl.CostEstimate(
            flops=10 * 10**9, bytes_accessed=20 * 10**6, transcendentals=0
        ),
    )(
        teacher_rows, teacher_gain.reshape(-1, 128), teacher_value,
        student_rows, student_gain.reshape(-1, 128), student_value, owners.reshape(1, blk),
    )
    return err, grad.astype(f32)


def solution(mesh):
    sizes = (mesh.shape["mp"], mesh.shape["role"], mesh.shape["rep"])
    return jax.shard_map(
        shards_fused if sizes == (4, 2, 2) else shards,
        mesh=mesh,
        in_specs=(
            P(("groups", "mp", "role"), "rep"),
            P("rep"),
            P("rep", "role"),
            P(("groups", "mp", "role"), "rep"),
            P("rep"),
            P("rep", "role"),
            P(("groups", "mp", "role"), None),
        ),
        out_specs=(P(("groups", "mp", "role"), "rep"), P(("groups", "rep"), "role")),
        check_vma=False,
    )
```
